32 devices in a mesh: grp: 4 (over y, x), ffn: 8 (over z, core).
Axes of the slice: x: 2, y: 2, z: 4, core: 2. Of those that a mesh axis runs over, the one named last changes fastest.
Arguments:
- layer_input: bfloat16 [288, 5120], P(None, 'ffn')
- norm_gain: float32 [5120], P('ffn'), may hold values from 0.1 to 1.9
- qkv_weight: bfloat16 [3, 5120, 2560], P(None, 'ffn', 'grp'), may hold values from -0.078125 to 0.078125
- key_cache: bfloat16 [880, 128, 2560], P('ffn', None, 'grp'), may hold values from -256 to 256
- value_cache: bfloat16 [880, 128, 2560], P('ffn', None, 'grp'), may hold values from -4 to 4
- out_weight: bfloat16 [2560, 5120], P('grp', 'ffn'), may hold values from -0.125 to 0.125
- ffn_gain: float32 [5120], replicated, may hold values from 0.1 to 1.9
- gate_up_weight: bfloat16 [2, 5120, 13824], P(None, None, 'ffn'), may hold values from -0.078125 to 0.078125
- down_weight: bfloat16 [13824, 5120], P('ffn'), may hold values from -0.0625 to 0.0625
- span_offsets: int32 [2], replicated, may hold values from 0 to 16256, as said below
- decode_lengths: int32 [32], replicated, may hold values from 1 to 16383, as said below
- page_table: int32 [34, 128], replicated, may hold values from -1 to 879, as said below
Outputs:
- layer_output: bfloat16 [288, 5120], P('grp', 'ffn')
The draws below stay inside these ranges and needn't reach their ends.
Inputs may be any that keep to these rules, and one draw needn't show every extreme that they name: `span_offsets`: the largest offset equals 16256. `decode_lengths`: one length equals 16383, the others are under 2048. `page_table`: row r holds page ids in its first ceil(n / 128) slots, where n is its prefix length plus its new tokens (128 for prefill, 1 for decode), and -1 in the others; no page id appears twice in the table.
All inputs are finite; a program needn't handle non-finite values.
Results may differ from the reference program's by a relative error of at most 0.025.
Values may be sent and summed in bfloat16 or wider, within the bound.
A program may use at most 320 MiB of HBM per device.

```python
import math
import jax
import jax.numpy as jnp
from jax import lax

D = 5120
HEADS = 20
HD = 128
FF = 13824
PAGE = 128
MAXLEN = 16384
SPAN = 128
PRE = 2
DEC = 32
DECAP = 2048
MAXP = 128
TOKENS = 288
PAGES = 880


def request_plan(key):
    key_offsets = jax.random.fold_in(key, 101)
    key_lengths = jax.random.fold_in(key, 102)
    key_order = jax.random.fold_in(key, 103)
    key_choose = jax.random.fold_in(key, 104)
    offsets = jax.random.randint(key_offsets, (PRE,), 0, MAXLEN - SPAN + 1)
    chosen = jax.random.randint(key_choose, (2,), 0, 1048576)
    offsets = jnp.where(jnp.arange(PRE) == chosen[0] % PRE, MAXLEN - SPAN, offsets)
    lengths = jax.random.randint(key_lengths, (DEC,), 1, DECAP)
    lengths = jnp.where(jnp.arange(DEC) == chosen[1] % DEC, MAXLEN - 1, lengths)
    needed = jnp.concatenate([(offsets + SPAN + PAGE - 1) // PAGE, (lengths + PAGE) // PAGE])
    starting = jnp.cumsum(needed) - needed
    ordering = jax.random.permutation(key_order, PAGES)
    leader = ordering[0]
    ordering = jnp.where(ordering == PAGES - 1, leader, jnp.where(ordering == leader, PAGES - 1, ordering))
    slot_index = jnp.arange(MAXP)[None, :]
    picked = ordering[jnp.clip(starting[:, None] + slot_index, 0, PAGES - 1)]
    table = jnp.where(slot_index < needed[:, None], picked, -1)
    return (offsets.astype(jnp.int32), lengths.astype(jnp.int32), table.astype(jnp.int32))


def draw_span_offsets(key, part):
    return request_plan(key)[0]


def draw_decode_lengths(key, part):
    return request_plan(key)[1]


def draw_page_table(key, part):
    return request_plan(key)[2]


def draw_layer_input(key, part):
    key_base, key_rows, key_cols = jax.random.split(key, 3)
    row_scale = jnp.exp(jax.random.uniform(key_rows, (TOKENS, 1), minval=math.log(0.4), maxval=math.log(2.5)))
    col_scale = jnp.exp(jax.random.uniform(key_cols, (1, D), minval=math.log(0.6), maxval=math.log(1.6)))
    ramp_scale = jnp.exp(math.log(3.0) * (jnp.arange(D, dtype=jnp.float32) / D - 0.5))[None, :]
    base = jnp.clip(jax.random.normal(key_base, (TOKENS, D)), -4.0, 4.0)
    return (base * row_scale * col_scale * ramp_scale).astype(jnp.bfloat16)


def draw_key_cache(key, part):
    key_base = jax.random.fold_in(key, 0)
    base = jnp.clip(jax.random.normal(key_base, (PAGES, PAGE, HEADS * HD)), -4.0, 4.0)
    return base.astype(jnp.bfloat16)


def draw_value_cache(key, part):
    key_mean, key_noise = jax.random.split(key, 2)
    centre = jax.random.normal(key_mean, (PAGES, 1, HEADS * HD))
    noise = 0.5 * jax.random.normal(key_noise, (PAGES, PAGE, HEADS * HD))
    return jnp.clip(centre + noise, -4.0, 4.0).astype(jnp.bfloat16)


def with_spikes(drawn, rng, source, target, parts, factor):
    def block_of(dim):
        return (jnp.arange(drawn.shape[dim]) // (drawn.shape[dim] // parts)).reshape((-1,) + (1,) * (drawn.ndim - 1 - dim))

    first = jax.random.permutation(rng, parts)[block_of(target)]
    second = (block_of(target) + parts // 2) % parts
    return jnp.where((block_of(source) == first) | (block_of(source) == second), factor * drawn, drawn)


def shard_levels(key, extent, pieces, least, top_value):
    factor_of = 1.0
    for axis_at, blocks in pieces:
        draws = jax.random.uniform(jax.random.fold_in(jax.random.fold_in(key, 6), axis_at), (blocks,), jnp.float32, least / len(pieces), top_value / len(pieces))
        factor_of = factor_of * jnp.repeat(jnp.exp(draws), extent[axis_at] // blocks).reshape((-1,) + (1,) * (len(extent) - 1 - axis_at))
    return factor_of


def gaussian(key, extent, spread, most, cuts=(), kind=jnp.bfloat16):
    level = shard_levels(key, extent, cuts, -0.22, 0.18) if cuts else 1.0
    result = jax.random.normal(key, extent, jnp.float32) * spread * level
    return jnp.minimum(jnp.maximum(result, -most), most).astype(kind)


def gaussian_with(rng, shape, deviation, bound, cuts, heavy, kind=jnp.bfloat16):
    result = deviation * jax.random.normal(rng, shape, jnp.float32)
    if cuts:
        result = result * shard_levels(rng, shape, cuts, -0.22, 0.18)
    return jnp.clip(with_spikes(result, jax.random.fold_in(rng, 3), *heavy), -bound, bound).astype(kind)


def setup_inputs(seed: int = 0) -> dict:
    keys = jax.random.split(jax.random.key(seed), 13)
    layer_input = draw_layer_input(jax.random.fold_in(keys[12], 71), 0)
    norm_gain = jnp.clip(1.0 + 0.18 * jax.random.normal(keys[1], (D,), jnp.float32), 0.1, 1.9)
    qkv_weight = gaussian(keys[2], (3, D, HEADS * HD), D ** -0.5, 0.078125, ((1, 8), (2, 4)))
    key_cache = draw_key_cache(jax.random.fold_in(keys[12], 71), 0)
    value_cache = draw_value_cache(jax.random.fold_in(keys[12], 71), 0)
    out_weight = gaussian(keys[5], (HEADS * HD, D), (HEADS * HD) ** -0.5, 0.125, ((0, 4), (1, 8)))
    ffn_gain = jnp.clip(1.0 + 0.18 * jax.random.normal(keys[6], (D,), jnp.float32), 0.1, 1.9)
    gate_up_weight = gaussian(keys[7], (2, D, FF), D ** -0.5, 0.078125, ((2, 8),))
    down_weight = gaussian_with(keys[8], (FF, D), FF ** -0.5, 0.0625, ((0, 8),), (0, 1, 8, 2.0))
    span_offsets = draw_span_offsets(jax.random.fold_in(keys[12], 71), 0)
    decode_lengths = draw_decode_lengths(jax.random.fold_in(keys[12], 71), 0)
    page_table = draw_page_table(jax.random.fold_in(keys[12], 71), 0)
    return {"layer_input": layer_input, "norm_gain": norm_gain, "qkv_weight": qkv_weight, "key_cache": key_cache, "value_cache": value_cache, "out_weight": out_weight, "ffn_gain": ffn_gain, "gate_up_weight": gate_up_weight, "down_weight": down_weight, "span_offsets": span_offsets, "decode_lengths": decode_lengths, "page_table": page_table}


EPS = 1e-05
NEG = -1e+30

def rotate(values, positions):
    half_width = values.shape[-1] // 2
    frequency = jnp.exp(jnp.arange(half_width, dtype=jnp.float32) * (-2.0 * math.log(10000.0) / values.shape[-1]))
    angles = positions.astype(jnp.float32)[:, None] * frequency[None, :]
    cosine = jnp.cos(angles)[:, None, :]
    sine_table = jnp.sin(angles)[:, None, :]
    leading = values[..., :half_width]
    trailing = values[..., half_width:]
    return jnp.concatenate([leading * cosine - trailing * sine_table, trailing * cosine + leading * sine_table], axis=-1)

def token_positions(span_offsets, decode_lengths):
    within = jnp.arange(SPAN, dtype=jnp.int32)
    prefill = (span_offsets[:, None] + within[None, :]).reshape(PRE * SPAN)
    return jnp.concatenate([prefill, decode_lengths]).astype(jnp.int32)

def request_keys(page_row, prefix_len, row_start, key_cache, value_cache, new_keys, new_values):
    key_positions = jnp.arange(MAXLEN, dtype=jnp.int32)
    page_ids = jnp.clip(page_row, 0, PAGES - 1).astype(jnp.int32)
    cached_keys = key_cache[page_ids].reshape(MAXLEN, HEADS, HD)
    cached_values = value_cache[page_ids].reshape(MAXLEN, HEADS, HD)
    key_rows = jnp.clip(row_start + key_positions - prefix_len, 0, TOKENS - 1).astype(jnp.int32)
    earlier = (key_positions < prefix_len)[:, None, None]
    return (jnp.where(earlier, cached_keys, new_keys[key_rows]), jnp.where(earlier, cached_values, new_values[key_rows]))

def head_attention(queries, query_positions, all_keys, all_values):
    key_positions = jnp.arange(MAXLEN, dtype=jnp.int32)
    visible = key_positions[None, :] <= query_positions[:, None]
    score_scale = HD ** (-0.5)

    def single_head(operands):
        head_queries, head_keys, head_values = operands
        scores = jnp.dot(head_queries, head_keys.T, preferred_element_type=jnp.float32) * score_scale
        capped = jnp.where(visible, scores, NEG)
        maxima = lax.optimization_barrier(jnp.max(capped, axis=1, keepdims=True))
        weights = jnp.where(visible, jnp.exp(capped - maxima), 0.0)
        totals = lax.optimization_barrier(jnp.sum(weights, axis=1, keepdims=True))
        return jnp.dot(weights.astype(jnp.bfloat16), head_values, preferred_element_type=jnp.float32) / totals
    outputs = lax.map(single_head, (jnp.swapaxes(queries, 0, 1), jnp.swapaxes(all_keys, 0, 1), jnp.swapaxes(all_values, 0, 1)))
    return jnp.swapaxes(outputs, 0, 1).reshape(queries.shape[0], HEADS * HD).astype(jnp.bfloat16)

def reference(layer_input, norm_gain, qkv_weight, key_cache, value_cache, out_weight, ffn_gain, gate_up_weight, down_weight, span_offsets, decode_lengths, page_table):
    input_f32 = layer_input.astype(jnp.float32)
    scaled = (input_f32 * norm_gain[None, :]).astype(jnp.bfloat16)
    inverse = lax.rsqrt(lax.optimization_barrier(jnp.sum(input_f32 * input_f32, axis=1)) / D + EPS)[:, None]
    positions = token_positions(span_offsets, decode_lengths)

    def project(which):
        projected = jnp.dot(scaled, qkv_weight[which], preferred_element_type=jnp.float32) * inverse
        return projected.reshape(TOKENS, HEADS, HD)
    queries = rotate(project(0), positions).astype(jnp.bfloat16)
    new_keys = rotate(project(1), positions).astype(jnp.bfloat16)
    new_values = project(2).astype(jnp.bfloat16)
    blocks = []
    for request in range(PRE):
        all_keys, all_values = request_keys(page_table[request], span_offsets[request], request * SPAN, key_cache, value_cache, new_keys, new_values)
        lower = request * SPAN
        blocks.append(head_attention(queries[lower:lower + SPAN], positions[lower:lower + SPAN], all_keys, all_values))

    def decode_one(operands):
        page_row, length, row_index = operands
        all_keys, all_values = request_keys(page_row, length, row_index, key_cache, value_cache, new_keys, new_values)
        query = lax.dynamic_slice_in_dim(queries, row_index, 1, 0)
        return head_attention(query, length[None], all_keys, all_values)[0]
    decode_rows = PRE * SPAN + jnp.arange(DEC, dtype=jnp.int32)
    blocks.append(lax.map(decode_one, (page_table[PRE:], decode_lengths, decode_rows)))
    heads_out = jnp.concatenate(blocks, axis=0)
    residual = (input_f32 + jnp.dot(heads_out, out_weight, preferred_element_type=jnp.float32)).astype(jnp.bfloat16)
    residual_f32 = residual.astype(jnp.float32)
    normed = (residual_f32 * lax.rsqrt(lax.optimization_barrier(jnp.sum(residual_f32 * residual_f32, axis=1)) / D + EPS)[:, None] * ffn_gain[None, :]).astype(jnp.bfloat16)
    gate = jnp.dot(normed, gate_up_weight[0], preferred_element_type=jnp.float32)
    up_part = jnp.dot(normed, gate_up_weight[1], preferred_element_type=jnp.float32)
    hidden = (jax.nn.silu(gate) * up_part).astype(jnp.bfloat16)
    return (residual_f32 + jnp.dot(hidden, down_weight, preferred_element_type=jnp.float32)).astype(jnp.bfloat16)
```

```python
import functools
import math

import jax
import jax.numpy as jnp
from jax import lax
from jax.experimental import pallas as pl
from jax.experimental.pallas import tpu as pltpu
from jax.sharding import PartitionSpec as P

D = 5120
HD = 128
PAGE = 128
SPAN = 128
PRE = 2
DEC = 32
MAXP = 128
TOKENS = 288


EPS = 1e-05
NEG = -1e30
SCALE = HD ** (-0.5)
GROUP = 4
SLOTS = 128
BUFFERS = 6
ROWS = 16


def rotate(values, positions):
    half_width = values.shape[-1] // 2
    frequency = jnp.exp(
        jnp.arange(half_width, dtype=jnp.float32) * (-2.0 * math.log(10000.0) / values.shape[-1])
    )
    angles = positions.astype(jnp.float32)[:, None] * frequency[None, :]
    cosine = jnp.cos(angles)[:, None, :]
    sine_table = jnp.sin(angles)[:, None, :]
    leading = values[..., :half_width]
    trailing = values[..., half_width:]
    return jnp.concatenate(
        [leading * cosine - trailing * sine_table, trailing * cosine + leading * sine_table],
        axis=-1,
    )


def token_positions(span_offsets, decode_lengths):
    within = jnp.arange(SPAN, dtype=jnp.int32)
    prefill = (span_offsets[:, None] + within[None, :]).reshape(PRE * SPAN)
    return jnp.concatenate([prefill, decode_lengths])


def finish_projection(summed, squares, positions, group_heads):
    inverse = lax.rsqrt(squares / D + EPS)[:, None]
    row_count = summed.shape[0]
    queries = rotate((summed[:, 0] * inverse).reshape(row_count, group_heads, HD), positions)
    fresh_keys = rotate((summed[:, 1] * inverse).reshape(row_count, group_heads, HD), positions)
    fresh_values = (summed[:, 2] * inverse).reshape(row_count, group_heads, HD)
    stacked = jnp.stack([queries, fresh_keys, fresh_values], axis=1).astype(jnp.bfloat16)
    return stacked.reshape(row_count, 3, group_heads * HD)


def split_bf16(value, pieces):
    out = []
    for _ in range(pieces):
        piece = value.astype(jnp.bfloat16).astype(jnp.float32)
        out.append(piece)
        value = value - piece
    return out


def attention_kernel(
    heads,
    plan,
    queries,
    new_keys,
    new_values,
    spread,
    start_m,
    start_l,
    start_o,
    key_cache,
    value_cache,
    packed,
    decode_out,
    decode_stats,
    key_buf,
    value_buf,
    run_m,
    run_l,
    run_o,
    dec_m,
    dec_l,
    dec_o,
    sems,
):
    end_first, end_prefill, end_all = plan[3, 0], plan[3, 1], plan[3, 2]

    def copies(group):
        place = lax.rem(group, BUFFERS)
        out = []
        for i in range(GROUP):
            page = plan[0, group * GROUP + i]
            out.append(
                pltpu.make_async_copy(
                    key_cache.at[page], key_buf.at[place, i], sems.at[place, 0, i]
                )
            )
            out.append(
                pltpu.make_async_copy(
                    value_cache.at[page], value_buf.at[place, i], sems.at[place, 1, i]
                )
            )
        return out

    def fetch(group):
        @pl.when(group < end_all)
        def _():
            for copy in copies(group):
                copy.start()

    for group in range(BUFFERS - 1):
        fetch(jnp.int32(group))

    run_m[...] = jnp.full_like(run_m, NEG)
    run_l[...] = jnp.zeros_like(run_l)
    run_o[...] = jnp.zeros_like(run_o)
    dec_m[...] = start_m[...]
    dec_l[...] = start_l[...]
    dec_o[...] = start_o[...]

    def prefill_step(request, head, keys, values, bias):
        columns = slice(head * HD, (head + 1) * HD)
        rows = pl.ds(pl.multiple_of(request * SPAN, SPAN), SPAN)
        scores = lax.dot_general(
            queries[rows, columns],
            keys,
            (((1,), (1,)), ((), ())),
            preferred_element_type=jnp.float32,
        )
        scores = scores + bias
        before = run_m[request, head]
        now = jnp.maximum(before, jnp.max(scores, axis=1, keepdims=True))
        fade = jnp.exp((before - now) * SCALE)
        weights = jnp.exp((scores - now[:, :1]) * SCALE)
        run_m[request, head] = now
        run_l[request, head] = run_l[request, head] * fade + jnp.sum(
            weights, axis=1, keepdims=True
        )
        run_o[request, head] = run_o[request, head] * fade + jnp.dot(
            weights.astype(jnp.bfloat16), values, preferred_element_type=jnp.float32
        )

    @pl.when(plan[3, 3] == 1)
    def _():
        causal = jnp.where(
            lax.broadcasted_iota(jnp.int32, (SPAN, SPAN), 1)
            <= lax.broadcasted_iota(jnp.int32, (SPAN, SPAN), 0),
            0.0,
            NEG,
        ).astype(jnp.float32)
        for request in range(PRE):
            rows = slice(request * SPAN, (request + 1) * SPAN)
            for head in range(heads):
                columns = slice(head * HD, (head + 1) * HD)
                prefill_step(
                    request, head, new_keys[rows, columns], new_values[rows, columns], causal
                )

    lanes = lax.broadcasted_iota(jnp.int32, (1, PAGE), 1)

    def prefill_group(group, place):
        request = (group >= end_first).astype(jnp.int32)
        bias = jnp.concatenate(
            [
                jnp.where(lanes < plan[1, group * GROUP + i], 0.0, NEG).astype(jnp.float32)
                for i in range(GROUP)
            ],
            axis=1,
        )
        for head in range(heads):
            columns = slice(head * HD, (head + 1) * HD)
            keys = key_buf[place, :, :, columns].reshape(GROUP * PAGE, HD)
            values = value_buf[place, :, :, columns].reshape(GROUP * PAGE, HD)
            prefill_step(request, head, keys, values, bias)

    def decode_group(group, place):
        row = lax.broadcasted_iota(jnp.int32, (8, HD), 0)
        parts = []
        for i in range(GROUP):
            scores = lax.dot_general(
                spread[plan[2, group * GROUP + i]],
                key_buf[place, i],
                (((1,), (1,)), ((), ())),
                preferred_element_type=jnp.float32,
            )
            valid = lanes < plan[1, group * GROUP + i]
            scores = jnp.where(valid, scores, NEG)
            top = jnp.max(scores, axis=1, keepdims=True)
            weights = jnp.where(valid, jnp.exp((scores - top) * SCALE), 0.0)
            total = jnp.sum(weights, axis=1, keepdims=True)
            product = jnp.dot(
                weights.astype(jnp.bfloat16),
                value_buf[place, i],
                preferred_element_type=jnp.float32,
            )
            value = jnp.zeros((8, HD), jnp.float32)
            for head in range(heads):
                value = jnp.where(row == head, product[:8, head * HD : (head + 1) * HD], value)
            parts.append((top[:8], total[:8], value))
        for i in range(GROUP):
            token = plan[2, group * GROUP + i]
            top, total, value = parts[i]
            before = dec_m[token]
            now = jnp.maximum(before, top)
            fade = jnp.exp((before - now) * SCALE)
            fresh = jnp.exp((top - now) * SCALE)
            dec_m[token] = now
            dec_l[token] = dec_l[token] * fade + total * fresh
            dec_o[token] = dec_o[token] * fade + value * fresh

    @pl.loop(0, end_all)
    def _(group):
        fetch(group + (BUFFERS - 1))
        for copy in copies(group):
            copy.wait()
        place = lax.rem(group, BUFFERS)

        @pl.when(group < end_prefill)
        def _():
            prefill_group(group, place)

        @pl.when(group >= end_prefill)
        def _():
            decode_group(group, place)

    width = heads * HD
    lane = lax.broadcasted_iota(jnp.int32, (SPAN, PAGE), 1)
    for request in range(PRE):
        rows = slice(request * SPAN, (request + 1) * SPAN)
        stats = jnp.zeros((SPAN, PAGE), jnp.float32)
        for head in range(heads):
            total = run_l[request, head]
            packed[rows, head * HD : (head + 1) * HD] = (
                run_o[request, head] / jnp.where(total > 0.0, total, 1.0)
            ).astype(jnp.bfloat16)
            pieces = split_bf16(run_m[request, head], 3) + split_bf16(total, 2)
            for j, piece in enumerate(pieces):
                stats = jnp.where(lane == head * 5 + j, piece, stats)
        packed[rows, width : width + PAGE] = stats.astype(jnp.bfloat16)
    total = dec_l[...]
    decode_out[...] = dec_o[...] / jnp.where(total > 0.0, total, 1.0)
    lane = lax.broadcasted_iota(jnp.int32, (DEC, 8, HD), 2)
    stats = jnp.zeros((DEC, 8, HD), jnp.float32)
    for j, piece in enumerate(split_bf16(dec_m[...], 3) + split_bf16(total, 2)):
        stats = jnp.where(lane == j, piece, stats)
    decode_stats[...] = stats


def attention(plan, queries, new_keys, new_values, key_cache, value_cache, first):
    width = queries.shape[1]
    heads = width // HD
    dec_q = queries[PRE * SPAN :]
    head_of = jnp.arange(width, dtype=jnp.int32) // HD
    own = head_of[None, :] == jnp.arange(ROWS, dtype=jnp.int32)[:, None]
    spread = jnp.where(own[None], dec_q[:, None, :], jnp.zeros((), dec_q.dtype))

    def by_head(rows):
        split = rows.astype(jnp.float32).reshape(DEC, heads, HD)
        return jnp.pad(split, ((0, 0), (0, 8 - heads), (0, 0)))

    self_score = jnp.sum(
        by_head(dec_q) * by_head(new_keys[PRE * SPAN :]), axis=2, keepdims=True
    )
    start_m = jnp.broadcast_to(jnp.where(first, self_score, NEG), (DEC, 8, HD))
    start_l = jnp.broadcast_to(jnp.where(first, 1.0, 0.0), (DEC, 8, HD)).astype(jnp.float32)
    start_o = jnp.where(first, by_head(new_values[PRE * SPAN :]), 0.0)
    vmem = pl.BlockSpec(memory_space=pltpu.VMEM)
    packed, decode_out, decode_stats = pl.pallas_call(
        functools.partial(attention_kernel, heads),
        out_shape=(
            jax.ShapeDtypeStruct((PRE * SPAN, width + PAGE), jnp.bfloat16),
            jax.ShapeDtypeStruct((DEC, 8, HD), jnp.float32),
            jax.ShapeDtypeStruct((DEC, 8, HD), jnp.float32),
        ),
        in_specs=[pl.BlockSpec(memory_space=pltpu.SMEM)]
        + [vmem] * 7
        + [pl.BlockSpec(memory_space=pl.ANY)] * 2,
        out_specs=(vmem, vmem, vmem),
        scratch_shapes=[
            pltpu.VMEM((BUFFERS, GROUP, PAGE, width), jnp.bfloat16),
            pltpu.VMEM((BUFFERS, GROUP, PAGE, width), jnp.bfloat16),
            pltpu.VMEM((PRE, heads, SPAN, HD), jnp.float32),
            pltpu.VMEM((PRE, heads, SPAN, HD), jnp.float32),
            pltpu.VMEM((PRE, heads, SPAN, HD), jnp.float32),
            pltpu.VMEM((DEC, 8, HD), jnp.float32),
            pltpu.VMEM((DEC, 8, HD), jnp.float32),
            pltpu.VMEM((DEC, 8, HD), jnp.float32),
            pltpu.SemaphoreType.DMA((BUFFERS, 2, GROUP)),
        ],
        compiler_params=pltpu.CompilerParams(vmem_limit_bytes=40 * 1024 * 1024),
        name="paged_attention",
    )(plan, queries, new_keys, new_values, spread, start_m, start_l, start_o, key_cache, value_cache)
    dec_rows = jnp.concatenate(
        [
            decode_out[:, :heads].reshape(DEC, width),
            jnp.pad(
                decode_stats[:, :heads, :5].reshape(DEC, heads * 5),
                ((0, 0), (0, PAGE - heads * 5)),
            ),
        ],
        axis=1,
    ).astype(jnp.bfloat16)
    return jnp.concatenate([packed, dec_rows], axis=0)


def page_plan(page_table, span_offsets, decode_lengths, first_page, page_count, first):
    local_ids = first_page + jnp.arange(page_count, dtype=jnp.int32)
    flat = page_table.reshape(-1)
    code = jnp.max(
        jnp.where(
            flat[None, :] == local_ids[:, None],
            jnp.arange(1, flat.shape[0] + 1, dtype=jnp.int32)[None, :],
            0,
        ),
        axis=1,
    )
    owner = (code - 1) // MAXP
    slot = (code - 1) % MAXP
    prefixes = jnp.concatenate([span_offsets, decode_lengths])
    request = jnp.arange(PRE + DEC, dtype=jnp.int32)
    prefix = jnp.sum(jnp.where(owner[:, None] == request[None, :], prefixes[None, :], 0), axis=1)
    count = jnp.where(code > 0, jnp.clip(prefix - slot * PAGE, 0, PAGE), 0)
    kind = jnp.where(count > 0, jnp.minimum(owner, PRE), PRE + 1)
    sizes = jnp.sum(kind[None, :] == jnp.arange(PRE + 1, dtype=jnp.int32)[:, None], axis=1)
    groups = (sizes + GROUP - 1) // GROUP
    ends = jnp.stack([groups[0], groups[0] + groups[1], groups[0] + groups[1] + groups[2]])
    begin = jnp.where(kind == 0, 0, jnp.where(kind == 1, ends[0], ends[1])) * GROUP
    index = jnp.arange(page_count, dtype=jnp.int32)
    rank = jnp.sum((kind[None, :] == kind[:, None]) & (index[None, :] < index[:, None]), axis=1)
    place = jnp.where(kind <= PRE, begin + rank, -1)
    hit = place[None, :] == jnp.arange(SLOTS, dtype=jnp.int32)[:, None]
    token = jnp.maximum(owner - PRE, 0)

    def listed(values):
        return jnp.sum(jnp.where(hit, values[None, :], 0), axis=1).astype(jnp.int32)

    last = jnp.concatenate([ends, first.astype(jnp.int32)[None]]).astype(jnp.int32)
    return jnp.stack(
        [listed(index), listed(count), listed(token), jnp.pad(last, (0, SLOTS - 4))]
    )


def join_parts(parts, heads):
    devices, tokens = parts.shape[0], parts.shape[1]
    width = heads * HD
    parts = parts.astype(jnp.float32)
    outs = parts[:, :, :width].reshape(devices, tokens, heads, HD)
    stats = parts[:, :, width : width + heads * 5].reshape(devices, tokens, heads, 5)
    maxima = stats[..., 0] + stats[..., 1] + stats[..., 2]
    share = (stats[..., 3] + stats[..., 4]) * jnp.exp((maxima - jnp.max(maxima, axis=0)) * SCALE)
    joined = jnp.sum(outs * share[..., None], axis=0) / jnp.sum(share, axis=0)[..., None]
    return joined.astype(jnp.bfloat16).reshape(tokens, width)


def shards(
    layer_input,
    norm_gain,
    qkv_weight,
    key_cache,
    value_cache,
    out_weight,
    ffn_gain,
    gate_up_weight,
    down_weight,
    span_offsets,
    decode_lengths,
    page_table,
):
    group_width = qkv_weight.shape[2]
    group_heads = group_width // HD
    n_ffn, n_grp = lax.axis_size("ffn"), lax.axis_size("grp")
    first = lax.axis_index("ffn") == 0
    page_count = key_cache.shape[0]
    plan = page_plan(
        page_table,
        span_offsets,
        decode_lengths,
        lax.axis_index("ffn") * page_count,
        page_count,
        first,
    )
    input_f32 = layer_input.astype(jnp.float32)
    scaled = (input_f32 * norm_gain[None, :]).astype(jnp.bfloat16)
    squares = jnp.sum(input_f32 * input_f32, axis=1)
    positions = token_positions(span_offsets, decode_lengths)
    partial_value = jnp.concatenate(
        [
            jnp.dot(scaled, qkv_weight[k], preferred_element_type=jnp.float32).astype(jnp.bfloat16)
            for k in range(3)
        ]
        + [jnp.broadcast_to(squares[:, None], (TOKENS, HD)).astype(jnp.bfloat16)],
        axis=1,
    )
    reduced = lax.psum(partial_value, "ffn").astype(jnp.float32)
    summed = reduced[:, : 3 * group_width].reshape(TOKENS, 3, group_width)
    fresh = finish_projection(summed, reduced[:, 3 * group_width], positions, group_heads)
    packed = attention(
        plan, fresh[:, 0], fresh[:, 1], fresh[:, 2], key_cache, value_cache, first
    )
    parts = lax.all_to_all(
        packed.reshape(n_ffn, TOKENS // n_ffn, packed.shape[1]), "ffn", 0, 0
    )
    heads_out = lax.all_gather(join_parts(parts, group_heads), "ffn", axis=0, tiled=True)
    head_part = jnp.dot(heads_out, out_weight, preferred_element_type=jnp.float32)
    quarter = TOKENS // n_grp
    blocks = lax.all_to_all(
        head_part.astype(jnp.bfloat16).reshape(n_grp, quarter, head_part.shape[1]), "grp", 0, 0
    )
    own_input = lax.dynamic_slice_in_dim(layer_input, lax.axis_index("grp") * quarter, quarter, 0)
    own_block = (
        own_input.astype(jnp.float32) + jnp.sum(blocks.astype(jnp.float32), axis=0)
    ).astype(jnp.bfloat16)
    block_rows = lax.all_gather(own_block, "ffn", axis=1, tiled=True)
    rows_f32 = block_rows.astype(jnp.float32)
    inverse = lax.rsqrt(jnp.sum(rows_f32 * rows_f32, axis=1) / D + EPS)[:, None]
    normed = (rows_f32 * inverse * ffn_gain[None, :]).astype(jnp.bfloat16)
    gate_up = jnp.einsum("td,kdf->ktf", normed, gate_up_weight, preferred_element_type=jnp.float32)
    hidden = (jax.nn.silu(gate_up[0]) * gate_up[1]).astype(jnp.bfloat16)
    down_terms = jnp.dot(hidden, down_weight, preferred_element_type=jnp.float32)
    pieces = lax.all_to_all(
        down_terms.astype(jnp.bfloat16).reshape(quarter, n_ffn, D // n_ffn).swapaxes(0, 1),
        "ffn",
        0,
        0,
    )
    summed_out = jnp.sum(pieces.astype(jnp.float32), axis=0)
    return (own_block.astype(jnp.float32) + summed_out).astype(jnp.bfloat16)


def solution(mesh):
    in_specs = (
        P(None, "ffn"),
        P("ffn"),
        P(None, "ffn", "grp"),
        P("ffn", None, "grp"),
        P("ffn", None, "grp"),
        P("grp", "ffn"),
        P(),
        P(None, None, "ffn"),
        P("ffn", None),
        P(),
        P(),
        P(),
    )
    out_specs = P("grp", "ffn")
    return jax.shard_map(shards, mesh=mesh, in_specs=in_specs, out_specs=out_specs, check_vma=False)
```

```python
import functools
import math

import jax
import jax.numpy as jnp
from jax import lax
from jax.experimental import pallas as pl
from jax.experimental.pallas import tpu as pltpu
from jax.sharding import PartitionSpec as P

D = 5120
HD = 128
PAGE = 128
SPAN = 128
PRE = 2
DEC = 32
MAXP = 128
TOKENS = 288


EPS = 1e-05
NEG = -1e30
SCALE = HD ** (-0.5)
GROUP = 4
SLOTS = 128
BUFFERS = 6
ROWS = 16


def rotary_tables(positions):
    frequency = jnp.exp(
        jnp.arange(HD // 2, dtype=jnp.float32) * (-2.0 * math.log(10000.0) / HD)
    )
    angles = positions.astype(jnp.float32)[:, None] * frequency[None, :]
    cosine, sine = jnp.cos(angles), jnp.sin(angles)
    return (
        jnp.concatenate([cosine, cosine], axis=1),
        jnp.concatenate([-sine, sine], axis=1),
    )


def token_positions(span_offsets, decode_lengths):
    within = jnp.arange(SPAN, dtype=jnp.int32)
    prefill = (span_offsets[:, None] + within[None, :]).reshape(PRE * SPAN)
    return jnp.concatenate([prefill, decode_lengths])


def pair_groups(n):
    return (
        [[2 * chip, 2 * chip + 1] for chip in range(n // 2)],
        [[2 * chip + core for chip in range(n // 2)] for core in range(2)],
    )


def scatter_sum(blocks):
    pairs, chips = pair_groups(lax.axis_size("ffn"))
    halves = lax.all_to_all(blocks, "ffn", 0, 0, axis_index_groups=pairs)
    half = jnp.sum(halves.astype(jnp.float32), axis=0).astype(blocks.dtype)
    parts = lax.all_to_all(half, "ffn", 0, 0, axis_index_groups=chips)
    return jnp.sum(parts.astype(jnp.float32), axis=0)


def split_bf16(value, pieces):
    out = []
    for _ in range(pieces):
        piece = value.astype(jnp.bfloat16).astype(jnp.float32)
        out.append(piece)
        value = value - piece
    return out


def attention_kernel(
    heads,
    plan,
    reduced,
    cosine,
    sine,
    key_cache,
    value_cache,
    packed,
    decode_out,
    decode_stats,
    queries,
    new_keys,
    new_values,
    spread,
    key_buf,
    value_buf,
    run_m,
    run_l,
    run_o,
    dec_m,
    dec_l,
    dec_o,
    sems,
):
    end_first, end_prefill, end_all = plan[3, 0], plan[3, 1], plan[3, 2]

    def copies(group):
        place = lax.rem(group, BUFFERS)
        out = []
        for i in range(GROUP):
            page = plan[0, group * GROUP + i]
            out.append(
                pltpu.make_async_copy(
                    key_cache.at[page], key_buf.at[place, i], sems.at[place, 0, i]
                )
            )
            out.append(
                pltpu.make_async_copy(
                    value_cache.at[page], value_buf.at[place, i], sems.at[place, 1, i]
                )
            )
        return out

    def fetch(group):
        @pl.when(group < end_all)
        def _():
            for copy in copies(group):
                copy.start()

    for group in range(BUFFERS - 1):
        fetch(jnp.int32(group))

    run_m[...] = jnp.full_like(run_m, NEG)
    run_l[...] = jnp.zeros_like(run_l)
    run_o[...] = jnp.zeros_like(run_o)

    width = heads * HD
    squares = reduced[:, 3 * width : 3 * width + HD].astype(jnp.float32)
    inverse = lax.rsqrt(squares / D + EPS)

    def projected(which, head):
        start = which * width + head * HD
        return reduced[:, start : start + HD].astype(jnp.float32) * inverse

    def turned(value):
        swapped = jnp.concatenate([value[:, HD // 2 :], value[:, : HD // 2]], axis=1)
        return value * cosine[...] + swapped * sine[...]

    is_first = plan[3, 3] == 1
    dec_row = lax.broadcasted_iota(jnp.int32, (DEC, 8, HD), 1)
    spread_row = lax.broadcasted_iota(jnp.int32, (DEC, ROWS, HD), 1)
    start_m = jnp.zeros((DEC, 8, HD), jnp.float32)
    start_o = jnp.zeros((DEC, 8, HD), jnp.float32)
    for head in range(heads):
        columns = slice(head * HD, (head + 1) * HD)
        query = turned(projected(0, head)).astype(jnp.bfloat16)
        key = turned(projected(1, head)).astype(jnp.bfloat16)
        value = projected(2, head).astype(jnp.bfloat16)
        queries[:, columns] = query
        new_keys[:, columns] = key
        new_values[:, columns] = value
        dec_q = query[PRE * SPAN :].astype(jnp.float32)
        dec_k = key[PRE * SPAN :].astype(jnp.float32)
        dec_v = value[PRE * SPAN :].astype(jnp.float32)
        spread[:, :, columns] = jnp.where(spread_row == head, dec_q[:, None, :], 0.0).astype(
            jnp.bfloat16
        )
        own = jnp.broadcast_to(jnp.sum(dec_q * dec_k, axis=1, keepdims=True), (DEC, HD))
        start_m = jnp.where(dec_row == head, own[:, None, :], start_m)
        start_o = jnp.where(dec_row == head, dec_v[:, None, :], start_o)
    dec_m[...] = jnp.where(is_first, start_m, NEG)
    dec_l[...] = jnp.full((DEC, 8, HD), jnp.where(is_first, 1.0, 0.0), jnp.float32)
    dec_o[...] = jnp.where(is_first, start_o, 0.0)

    def prefill_step(request, head, keys, values, bias):
        columns = slice(head * HD, (head + 1) * HD)
        rows = pl.ds(pl.multiple_of(request * SPAN, SPAN), SPAN)
        scores = lax.dot_general(
            queries[rows, columns],
            keys,
            (((1,), (1,)), ((), ())),
            preferred_element_type=jnp.float32,
        )
        scores = scores + bias
        before = run_m[request, head]
        now = jnp.maximum(before, jnp.max(scores, axis=1, keepdims=True))
        fade = jnp.exp((before - now) * SCALE)
        weights = jnp.exp((scores - now[:, :1]) * SCALE)
        run_m[request, head] = now
        run_l[request, head] = run_l[request, head] * fade + jnp.sum(
            weights, axis=1, keepdims=True
        )
        run_o[request, head] = run_o[request, head] * fade + jnp.dot(
            weights.astype(jnp.bfloat16), values, preferred_element_type=jnp.float32
        )

    @pl.when(plan[3, 3] == 1)
    def _():
        causal = jnp.where(
            lax.broadcasted_iota(jnp.int32, (SPAN, SPAN), 1)
            <= lax.broadcasted_iota(jnp.int32, (SPAN, SPAN), 0),
            0.0,
            NEG,
        ).astype(jnp.float32)
        for request in range(PRE):
            rows = slice(request * SPAN, (request + 1) * SPAN)
            for head in range(heads):
                columns = slice(head * HD, (head + 1) * HD)
                prefill_step(
                    request, head, new_keys[rows, columns], new_values[rows, columns], causal
                )

    lanes = lax.broadcasted_iota(jnp.int32, (1, PAGE), 1)

    def prefill_group(group, place):
        request = (group >= end_first).astype(jnp.int32)
        bias = jnp.concatenate(
            [
                jnp.where(lanes < plan[1, group * GROUP + i], 0.0, NEG).astype(jnp.float32)
                for i in range(GROUP)
            ],
            axis=1,
        )
        for head in range(heads):
            columns = slice(head * HD, (head + 1) * HD)
            keys = key_buf[place, :, :, columns].reshape(GROUP * PAGE, HD)
            values = value_buf[place, :, :, columns].reshape(GROUP * PAGE, HD)
            prefill_step(request, head, keys, values, bias)

    def decode_group(group, place):
        row = lax.broadcasted_iota(jnp.int32, (8, HD), 0)
        parts = []
        for i in range(GROUP):
            scores = lax.dot_general(
                spread[plan[2, group * GROUP + i]],
                key_buf[place, i],
                (((1,), (1,)), ((), ())),
                preferred_element_type=jnp.float32,
            )
            valid = lanes < plan[1, group * GROUP + i]
            scores = jnp.where(valid, scores, NEG)
            top = jnp.max(scores, axis=1, keepdims=True)
            weights = jnp.where(valid, jnp.exp((scores - top) * SCALE), 0.0)
            total = jnp.sum(weights, axis=1, keepdims=True)
            product = jnp.dot(
                weights.astype(jnp.bfloat16),
                value_buf[place, i],
                preferred_element_type=jnp.float32,
            )
            value = jnp.zeros((8, HD), jnp.float32)
            for head in range(heads):
                value = jnp.where(row == head, product[:8, head * HD : (head + 1) * HD], value)
            parts.append((top[:8], total[:8], value))
        for i in range(GROUP):
            token = plan[2, group * GROUP + i]
            top, total, value = parts[i]
            before = dec_m[token]
            now = jnp.maximum(before, top)
            fade = jnp.exp((before - now) * SCALE)
            fresh = jnp.exp((top - now) * SCALE)
            dec_m[token] = now
            dec_l[token] = dec_l[token] * fade + total * fresh
            dec_o[token] = dec_o[token] * fade + value * fresh

    @pl.loop(0, end_all)
    def _(group):
        fetch(group + (BUFFERS - 1))
        for copy in copies(group):
            copy.wait()
        place = lax.rem(group, BUFFERS)

        @pl.when(group < end_prefill)
        def _():
            prefill_group(group, place)

        @pl.when(group >= end_prefill)
        def _():
            decode_group(group, place)

    lane = lax.broadcasted_iota(jnp.int32, (SPAN, PAGE), 1)
    for request in range(PRE):
        rows = slice(request * SPAN, (request + 1) * SPAN)
        stats = jnp.zeros((SPAN, PAGE), jnp.float32)
        for head in range(heads):
            total = run_l[request, head]
            packed[rows, head * HD : (head + 1) * HD] = (
                run_o[request, head] / jnp.where(total > 0.0, total, 1.0)
            ).astype(jnp.bfloat16)
            pieces = split_bf16(run_m[request, head], 3) + split_bf16(total, 2)
            for j, piece in enumerate(pieces):
                stats = jnp.where(lane == head * 5 + j, piece, stats)
        packed[rows, width : width + PAGE] = stats.astype(jnp.bfloat16)
    total = dec_l[...]
    decode_out[...] = dec_o[...] / jnp.where(total > 0.0, total, 1.0)
    lane = lax.broadcasted_iota(jnp.int32, (DEC, 8, HD), 2)
    stats = jnp.zeros((DEC, 8, HD), jnp.float32)
    for j, piece in enumerate(split_bf16(dec_m[...], 3) + split_bf16(total, 2)):
        stats = jnp.where(lane == j, piece, stats)
    decode_stats[...] = stats


def attention(plan, reduced, positions, key_cache, value_cache):
    width = key_cache.shape[2]
    heads = width // HD
    cosine, sine = rotary_tables(positions)
    vmem = pl.BlockSpec(memory_space=pltpu.VMEM)
    packed, decode_out, decode_stats = pl.pallas_call(
        functools.partial(attention_kernel, heads),
        out_shape=(
            jax.ShapeDtypeStruct((PRE * SPAN, width + PAGE), jnp.bfloat16),
            jax.ShapeDtypeStruct((DEC, 8, HD), jnp.float32),
            jax.ShapeDtypeStruct((DEC, 8, HD), jnp.float32),
        ),
        in_specs=[pl.BlockSpec(memory_space=pltpu.SMEM)]
        + [vmem] * 3
        + [pl.BlockSpec(memory_space=pl.ANY)] * 2,
        out_specs=(vmem, vmem, vmem),
        scratch_shapes=[
            pltpu.VMEM((TOKENS, width), jnp.bfloat16),
            pltpu.VMEM((TOKENS, width), jnp.bfloat16),
            pltpu.VMEM((TOKENS, width), jnp.bfloat16),
            pltpu.VMEM((DEC, ROWS, width), jnp.bfloat16),
            pltpu.VMEM((BUFFERS, GROUP, PAGE, width), jnp.bfloat16),
            pltpu.VMEM((BUFFERS, GROUP, PAGE, width), jnp.bfloat16),
            pltpu.VMEM((PRE, heads, SPAN, HD), jnp.float32),
            pltpu.VMEM((PRE, heads, SPAN, HD), jnp.float32),
            pltpu.VMEM((PRE, heads, SPAN, HD), jnp.float32),
            pltpu.VMEM((DEC, 8, HD), jnp.float32),
            pltpu.VMEM((DEC, 8, HD), jnp.float32),
            pltpu.VMEM((DEC, 8, HD), jnp.float32),
            pltpu.SemaphoreType.DMA((BUFFERS, 2, GROUP)),
        ],
        compiler_params=pltpu.CompilerParams(vmem_limit_bytes=40 * 1024 * 1024),
        name="paged_attention",
    )(plan, reduced, cosine, sine, key_cache, value_cache)
    dec_rows = jnp.concatenate(
        [
            decode_out[:, :heads].reshape(DEC, width),
            jnp.pad(
                decode_stats[:, :heads, :5].reshape(DEC, heads * 5),
                ((0, 0), (0, PAGE - heads * 5)),
            ),
        ],
        axis=1,
    ).astype(jnp.bfloat16)
    return jnp.concatenate([packed, dec_rows], axis=0)


def page_plan(page_table, span_offsets, decode_lengths, first_page, page_count, first):
    local_ids = first_page + jnp.arange(page_count, dtype=jnp.int32)
    flat = page_table.reshape(-1)
    code = jnp.max(
        jnp.where(
            flat[None, :] == local_ids[:, None],
            jnp.arange(1, flat.shape[0] + 1, dtype=jnp.int32)[None, :],
            0,
        ),
        axis=1,
    )
    owner = (code - 1) // MAXP
    slot = (code - 1) % MAXP
    prefixes = jnp.concatenate([span_offsets, decode_lengths])
    request = jnp.arange(PRE + DEC, dtype=jnp.int32)
    prefix = jnp.sum(jnp.where(owner[:, None] == request[None, :], prefixes[None, :], 0), axis=1)
    count = jnp.where(code > 0, jnp.clip(prefix - slot * PAGE, 0, PAGE), 0)
    kind = jnp.where(count > 0, jnp.minimum(owner, PRE), PRE + 1)
    sizes = jnp.sum(kind[None, :] == jnp.arange(PRE + 1, dtype=jnp.int32)[:, None], axis=1)
    groups = (sizes + GROUP - 1) // GROUP
    ends = jnp.stack([groups[0], groups[0] + groups[1], groups[0] + groups[1] + groups[2]])
    begin = jnp.where(kind == 0, 0, jnp.where(kind == 1, ends[0], ends[1])) * GROUP
    index = jnp.arange(page_count, dtype=jnp.int32)
    rank = jnp.sum((kind[None, :] == kind[:, None]) & (index[None, :] < index[:, None]), axis=1)
    place = jnp.where(kind <= PRE, begin + rank, -1)
    hit = place[None, :] == jnp.arange(SLOTS, dtype=jnp.int32)[:, None]
    token = jnp.maximum(owner - PRE, 0)

    def listed(values):
        return jnp.sum(jnp.where(hit, values[None, :], 0), axis=1).astype(jnp.int32)

    last = jnp.concatenate([ends, first.astype(jnp.int32)[None]]).astype(jnp.int32)
    return jnp.stack(
        [listed(index), listed(count), listed(token), jnp.pad(last, (0, SLOTS - 4))]
    )


def join_parts(parts, heads):
    devices, tokens = parts.shape[0], parts.shape[1]
    width = heads * HD
    parts = parts.astype(jnp.float32)
    outs = parts[:, :, :width].reshape(devices, tokens, heads, HD)
    stats = parts[:, :, width : width + heads * 5].reshape(devices, tokens, heads, 5)
    maxima = stats[..., 0] + stats[..., 1] + stats[..., 2]
    share = (stats[..., 3] + stats[..., 4]) * jnp.exp((maxima - jnp.max(maxima, axis=0)) * SCALE)
    joined = jnp.sum(outs * share[..., None], axis=0) / jnp.sum(share, axis=0)[..., None]
    return joined.astype(jnp.bfloat16).reshape(tokens, width)


def shards(
    layer_input,
    norm_gain,
    qkv_weight,
    key_cache,
    value_cache,
    out_weight,
    ffn_gain,
    gate_up_weight,
    down_weight,
    span_offsets,
    decode_lengths,
    page_table,
):
    group_width = qkv_weight.shape[2]
    group_heads = group_width // HD
    n_ffn, n_grp = lax.axis_size("ffn"), lax.axis_size("grp")
    first = lax.axis_index("ffn") == 0
    page_count = key_cache.shape[0]
    plan = page_plan(
        page_table,
        span_offsets,
        decode_lengths,
        lax.axis_index("ffn") * page_count,
        page_count,
        first,
    )
    input_f32 = layer_input.astype(jnp.float32)
    scaled = (input_f32 * norm_gain[None, :]).astype(jnp.bfloat16)
    squares = jnp.sum(input_f32 * input_f32, axis=1)
    positions = token_positions(span_offsets, decode_lengths)
    partial_value = jnp.concatenate(
        [
            jnp.dot(scaled, qkv_weight[k], preferred_element_type=jnp.float32).astype(jnp.bfloat16)
            for k in range(3)
        ]
        + [jnp.broadcast_to(squares[:, None], (TOKENS, HD)).astype(jnp.bfloat16)],
        axis=1,
    )
    pairs, chips = pair_groups(n_ffn)
    columns = partial_value.shape[1] // n_ffn
    own_sum = scatter_sum(
        partial_value.reshape(TOKENS, 2, n_ffn // 2, columns).transpose(1, 2, 0, 3)
    ).astype(jnp.bfloat16)
    of_core = lax.all_gather(own_sum, "ffn", axis_index_groups=chips)
    gathered = lax.all_gather(of_core, "ffn", axis_index_groups=pairs)
    reduced = gathered.transpose(2, 0, 1, 3).reshape(partial_value.shape)
    packed = attention(plan, reduced, positions, key_cache, value_cache)
    parts = lax.all_to_all(
        packed.reshape(n_ffn, TOKENS // n_ffn, packed.shape[1]), "ffn", 0, 0
    )
    heads_out = lax.all_gather(join_parts(parts, group_heads), "ffn", axis=0, tiled=True)
    head_part = jnp.dot(heads_out, out_weight, preferred_element_type=jnp.float32)
    quarter = TOKENS // n_grp
    blocks = lax.all_to_all(
        head_part.astype(jnp.bfloat16).reshape(n_grp, quarter, head_part.shape[1]), "grp", 0, 0
    )
    own_input = lax.dynamic_slice_in_dim(layer_input, lax.axis_index("grp") * quarter, quarter, 0)
    own_block = (
        own_input.astype(jnp.float32) + jnp.sum(blocks.astype(jnp.float32), axis=0)
    ).astype(jnp.bfloat16)
    block_rows = lax.all_gather(own_block, "ffn", axis=1, tiled=True)
    rows_f32 = block_rows.astype(jnp.float32)
    inverse = lax.rsqrt(jnp.sum(rows_f32 * rows_f32, axis=1) / D + EPS)[:, None]
    normed = (rows_f32 * inverse * ffn_gain[None, :]).astype(jnp.bfloat16)
    gate_up = jnp.einsum("td,kdf->ktf", normed, gate_up_weight, preferred_element_type=jnp.float32)
    hidden = (jax.nn.silu(gate_up[0]) * gate_up[1]).astype(jnp.bfloat16)
    down_terms = jnp.dot(hidden, down_weight, preferred_element_type=jnp.float32)
    summed_out = scatter_sum(
        down_terms.astype(jnp.bfloat16)
        .reshape(quarter, n_ffn // 2, 2, D // n_ffn)
        .transpose(2, 1, 0, 3)
    )
    return (own_block.astype(jnp.float32) + summed_out).astype(jnp.bfloat16)


def solution(mesh):
    in_specs = (
        P(None, "ffn"),
        P("ffn"),
        P(None, "ffn", "grp"),
        P("ffn", None, "grp"),
        P("ffn", None, "grp"),
        P("grp", "ffn"),
        P(),
        P(None, None, "ffn"),
        P("ffn", None),
        P(),
        P(),
        P(),
    )
    out_specs = P("grp", "ffn")
    return jax.shard_map(shards, mesh=mesh, in_specs=in_specs, out_specs=out_specs, check_vma=False)
```

```python
import functools
import math

import jax
import jax.numpy as jnp
from jax import lax
from jax.experimental import pallas as pl
from jax.experimental.pallas import tpu as pltpu
from jax.sharding import PartitionSpec as P

D = 5120
HD = 128
PAGE = 128
SPAN = 128
PRE = 2
DEC = 32
MAXP = 128
TOKENS = 288


EPS = 1e-05
NEG = -1e30
SCALE = HD ** (-0.5)
GROUP = 4
SLOTS = 128
BUFFERS = 6
ROWS = 16


def rotary_tables(positions):
    frequency = jnp.exp(
        jnp.arange(HD // 2, dtype=jnp.float32) * (-2.0 * math.log(10000.0) / HD)
    )
    angles = positions.astype(jnp.float32)[:, None] * frequency[None, :]
    cosine, sine = jnp.cos(angles), jnp.sin(angles)
    return (
        jnp.concatenate([cosine, cosine], axis=1),
        jnp.concatenate([-sine, sine], axis=1),
    )


def token_positions(span_offsets, decode_lengths):
    within = jnp.arange(SPAN, dtype=jnp.int32)
    prefill = (span_offsets[:, None] + within[None, :]).reshape(PRE * SPAN)
    return jnp.concatenate([prefill, decode_lengths])


def pair_groups(n):
    return (
        [[2 * chip, 2 * chip + 1] for chip in range(n // 2)],
        [[2 * chip + core for chip in range(n // 2)] for core in range(2)],
    )


def scatter_sum(blocks):
    pairs, chips = pair_groups(lax.axis_size("ffn"))
    halves = lax.all_to_all(blocks, "ffn", 0, 0, axis_index_groups=pairs)
    half = jnp.sum(halves.astype(jnp.float32), axis=0).astype(blocks.dtype)
    parts = lax.all_to_all(half, "ffn", 0, 0, axis_index_groups=chips)
    return jnp.sum(parts.astype(jnp.float32), axis=0)


def gather_all(block):
    n = lax.axis_size("ffn")
    mine = lax.all_gather(block, "ffn", axis_index_groups=pair_groups(n)[1])
    other = lax.ppermute(mine, "ffn", [(i, i ^ 1) for i in range(n)])
    even = lax.axis_index("ffn") % 2 == 0
    return jnp.stack([jnp.where(even, mine, other), jnp.where(even, other, mine)])


def split_bf16(value, pieces):
    out = []
    for _ in range(pieces):
        piece = value.astype(jnp.bfloat16).astype(jnp.float32)
        out.append(piece)
        value = value - piece
    return out


def attention_kernel(
    heads,
    plan,
    reduced,
    cosine,
    sine,
    key_cache,
    value_cache,
    packed,
    decode_out,
    decode_stats,
    queries,
    new_keys,
    new_values,
    spread,
    key_buf,
    value_buf,
    run_m,
    run_l,
    run_o,
    dec_m,
    dec_l,
    dec_o,
    sems,
):
    end_first, end_prefill, end_all = plan[3, 0], plan[3, 1], plan[3, 2]

    def copies(group):
        place = lax.rem(group, BUFFERS)
        out = []
        for i in range(GROUP):
            page = plan[0, group * GROUP + i]
            out.append(
                pltpu.make_async_copy(
                    key_cache.at[page], key_buf.at[place, i], sems.at[place, 0, i]
                )
            )
            out.append(
                pltpu.make_async_copy(
                    value_cache.at[page], value_buf.at[place, i], sems.at[place, 1, i]
                )
            )
        return out

    def fetch(group):
        @pl.when(group < end_all)
        def _():
            for copy in copies(group):
                copy.start()

    for group in range(BUFFERS - 1):
        fetch(jnp.int32(group))

    run_m[...] = jnp.full_like(run_m, NEG)
    run_l[...] = jnp.zeros_like(run_l)
    run_o[...] = jnp.zeros_like(run_o)

    width = heads * HD
    block = reduced.shape[2]

    def lanes_at(start):
        offset = start % block
        return reduced[start // block, :, offset : offset + HD].astype(jnp.float32)

    squares = lanes_at(3 * width)
    inverse = lax.rsqrt(squares / D + EPS)

    def projected(which, head):
        return lanes_at(which * width + head * HD) * inverse

    def turned(value):
        swapped = jnp.concatenate([value[:, HD // 2 :], value[:, : HD // 2]], axis=1)
        return value * cosine[...] + swapped * sine[...]

    is_first = plan[3, 3] == 1
    dec_row = lax.broadcasted_iota(jnp.int32, (DEC, 8, HD), 1)
    spread_row = lax.broadcasted_iota(jnp.int32, (DEC, ROWS, HD), 1)
    start_m = jnp.zeros((DEC, 8, HD), jnp.float32)
    start_o = jnp.zeros((DEC, 8, HD), jnp.float32)
    for head in range(heads):
        columns = slice(head * HD, (head + 1) * HD)
        query = turned(projected(0, head)).astype(jnp.bfloat16)
        key = turned(projected(1, head)).astype(jnp.bfloat16)
        value = projected(2, head).astype(jnp.bfloat16)
        queries[:, columns] = query
        new_keys[:, columns] = key
        new_values[:, columns] = value
        dec_q = query[PRE * SPAN :].astype(jnp.float32)
        dec_k = key[PRE * SPAN :].astype(jnp.float32)
        dec_v = value[PRE * SPAN :].astype(jnp.float32)
        spread[:, :, columns] = jnp.where(spread_row == head, dec_q[:, None, :], 0.0).astype(
            jnp.bfloat16
        )
        own = jnp.broadcast_to(jnp.sum(dec_q * dec_k, axis=1, keepdims=True), (DEC, HD))
        start_m = jnp.where(dec_row == head, own[:, None, :], start_m)
        start_o = jnp.where(dec_row == head, dec_v[:, None, :], start_o)
    dec_m[...] = jnp.where(is_first, start_m, NEG)
    dec_l[...] = jnp.full((DEC, 8, HD), jnp.where(is_first, 1.0, 0.0), jnp.float32)
    dec_o[...] = jnp.where(is_first, start_o, 0.0)

    def prefill_step(request, head, keys, values, bias):
        columns = slice(head * HD, (head + 1) * HD)
        rows = pl.ds(pl.multiple_of(request * SPAN, SPAN), SPAN)
        scores = lax.dot_general(
            queries[rows, columns],
            keys,
            (((1,), (1,)), ((), ())),
            preferred_element_type=jnp.float32,
        )
        scores = scores + bias
        before = run_m[request, head]
        now = jnp.maximum(before, jnp.max(scores, axis=1, keepdims=True))
        fade = jnp.exp((before - now) * SCALE)
        weights = jnp.exp((scores - now[:, :1]) * SCALE)
        run_m[request, head] = now
        run_l[request, head] = run_l[request, head] * fade + jnp.sum(
            weights, axis=1, keepdims=True
        )
        run_o[request, head] = run_o[request, head] * fade + jnp.dot(
            weights.astype(jnp.bfloat16), values, preferred_element_type=jnp.float32
        )

    @pl.when(plan[3, 3] == 1)
    def _():
        causal = jnp.where(
            lax.broadcasted_iota(jnp.int32, (SPAN, SPAN), 1)
            <= lax.broadcasted_iota(jnp.int32, (SPAN, SPAN), 0),
            0.0,
            NEG,
        ).astype(jnp.float32)
        for request in range(PRE):
            rows = slice(request * SPAN, (request + 1) * SPAN)
            for head in range(heads):
                columns = slice(head * HD, (head + 1) * HD)
                prefill_step(
                    request, head, new_keys[rows, columns], new_values[rows, columns], causal
                )

    lanes = lax.broadcasted_iota(jnp.int32, (1, PAGE), 1)

    def prefill_group(group, place):
        request = (group >= end_first).astype(jnp.int32)
        bias = jnp.concatenate(
            [
                jnp.where(lanes < plan[1, group * GROUP + i], 0.0, NEG).astype(jnp.float32)
                for i in range(GROUP)
            ],
            axis=1,
        )
        for head in range(heads):
            columns = slice(head * HD, (head + 1) * HD)
            keys = key_buf[place, :, :, columns].reshape(GROUP * PAGE, HD)
            values = value_buf[place, :, :, columns].reshape(GROUP * PAGE, HD)
            prefill_step(request, head, keys, values, bias)

    def decode_group(group, place):
        row = lax.broadcasted_iota(jnp.int32, (8, HD), 0)
        parts = []
        for i in range(GROUP):
            scores = lax.dot_general(
                spread[plan[2, group * GROUP + i]],
                key_buf[place, i],
                (((1,), (1,)), ((), ())),
                preferred_element_type=jnp.float32,
            )
            valid = lanes < plan[1, group * GROUP + i]
            scores = jnp.where(valid, scores, NEG)
            top = jnp.max(scores, axis=1, keepdims=True)
            weights = jnp.where(valid, jnp.exp((scores - top) * SCALE), 0.0)
            total = jnp.sum(weights, axis=1, keepdims=True)
            product = jnp.dot(
                weights.astype(jnp.bfloat16),
                value_buf[place, i],
                preferred_element_type=jnp.float32,
            )
            value = jnp.zeros((8, HD), jnp.float32)
            for head in range(heads):
                value = jnp.where(row == head, product[:8, head * HD : (head + 1) * HD], value)
            parts.append((top[:8], total[:8], value))
        for i in range(GROUP):
            token = plan[2, group * GROUP + i]
            top, total, value = parts[i]
            before = dec_m[token]
            now = jnp.maximum(before, top)
            fade = jnp.exp((before - now) * SCALE)
            fresh = jnp.exp((top - now) * SCALE)
            dec_m[token] = now
            dec_l[token] = dec_l[token] * fade + total * fresh
            dec_o[token] = dec_o[token] * fade + value * fresh

    @pl.loop(0, end_all)
    def _(group):
        fetch(group + (BUFFERS - 1))
        for copy in copies(group):
            copy.wait()
        place = lax.rem(group, BUFFERS)

        @pl.when(group < end_prefill)
        def _():
            prefill_group(group, place)

        @pl.when(group >= end_prefill)
        def _():
            decode_group(group, place)

    lane = lax.broadcasted_iota(jnp.int32, (SPAN, PAGE), 1)
    for request in range(PRE):
        rows = slice(request * SPAN, (request + 1) * SPAN)
        stats = jnp.zeros((SPAN, PAGE), jnp.float32)
        for head in range(heads):
            total = run_l[request, head]
            packed[rows, head * HD : (head + 1) * HD] = (
                run_o[request, head] / jnp.where(total > 0.0, total, 1.0)
            ).astype(jnp.bfloat16)
            pieces = split_bf16(run_m[request, head], 3) + split_bf16(total, 2)
            for j, piece in enumerate(pieces):
                stats = jnp.where(lane == head * 5 + j, piece, stats)
        packed[rows, width : width + PAGE] = stats.astype(jnp.bfloat16)
    total = dec_l[...]
    decode_out[...] = dec_o[...] / jnp.where(total > 0.0, total, 1.0)
    lane = lax.broadcasted_iota(jnp.int32, (DEC, 8, HD), 2)
    stats = jnp.zeros((DEC, 8, HD), jnp.float32)
    for j, piece in enumerate(split_bf16(dec_m[...], 3) + split_bf16(total, 2)):
        stats = jnp.where(lane == j, piece, stats)
    decode_stats[...] = stats


def attention(plan, reduced, positions, key_cache, value_cache):
    width = key_cache.shape[2]
    heads = width // HD
    cosine, sine = rotary_tables(positions)
    vmem = pl.BlockSpec(memory_space=pltpu.VMEM)
    packed, decode_out, decode_stats = pl.pallas_call(
        functools.partial(attention_kernel, heads),
        out_shape=(
            jax.ShapeDtypeStruct((PRE * SPAN, width + PAGE), jnp.bfloat16),
            jax.ShapeDtypeStruct((DEC, 8, HD), jnp.float32),
            jax.ShapeDtypeStruct((DEC, 8, HD), jnp.float32),
        ),
        in_specs=[pl.BlockSpec(memory_space=pltpu.SMEM)]
        + [vmem] * 3
        + [pl.BlockSpec(memory_space=pl.ANY)] * 2,
        out_specs=(vmem, vmem, vmem),
        scratch_shapes=[
            pltpu.VMEM((TOKENS, width), jnp.bfloat16),
            pltpu.VMEM((TOKENS, width), jnp.bfloat16),
            pltpu.VMEM((TOKENS, width), jnp.bfloat16),
            pltpu.VMEM((DEC, ROWS, width), jnp.bfloat16),
            pltpu.VMEM((BUFFERS, GROUP, PAGE, width), jnp.bfloat16),
            pltpu.VMEM((BUFFERS, GROUP, PAGE, width), jnp.bfloat16),
            pltpu.VMEM((PRE, heads, SPAN, HD), jnp.float32),
            pltpu.VMEM((PRE, heads, SPAN, HD), jnp.float32),
            pltpu.VMEM((PRE, heads, SPAN, HD), jnp.float32),
            pltpu.VMEM((DEC, 8, HD), jnp.float32),
            pltpu.VMEM((DEC, 8, HD), jnp.float32),
            pltpu.VMEM((DEC, 8, HD), jnp.float32),
            pltpu.SemaphoreType.DMA((BUFFERS, 2, GROUP)),
        ],
        compiler_params=pltpu.CompilerParams(vmem_limit_bytes=40 * 1024 * 1024),
        name="paged_attention",
    )(plan, reduced, cosine, sine, key_cache, value_cache)
    dec_rows = jnp.concatenate(
        [
            decode_out[:, :heads].reshape(DEC, width),
            jnp.pad(
                decode_stats[:, :heads, :5].reshape(DEC, heads * 5),
                ((0, 0), (0, PAGE - heads * 5)),
            ),
        ],
        axis=1,
    ).astype(jnp.bfloat16)
    return jnp.concatenate([packed, dec_rows], axis=0)


def page_plan(page_table, span_offsets, decode_lengths, first_page, page_count, first):
    local_ids = first_page + jnp.arange(page_count, dtype=jnp.int32)
    flat = page_table.reshape(-1)
    code = jnp.max(
        jnp.where(
            flat[None, :] == local_ids[:, None],
            jnp.arange(1, flat.shape[0] + 1, dtype=jnp.int32)[None, :],
            0,
        ),
        axis=1,
    )
    owner = (code - 1) // MAXP
    slot = (code - 1) % MAXP
    prefixes = jnp.concatenate([span_offsets, decode_lengths])
    request = jnp.arange(PRE + DEC, dtype=jnp.int32)
    prefix = jnp.sum(jnp.where(owner[:, None] == request[None, :], prefixes[None, :], 0), axis=1)
    count = jnp.where(code > 0, jnp.clip(prefix - slot * PAGE, 0, PAGE), 0)
    kind = jnp.where(count > 0, jnp.minimum(owner, PRE), PRE + 1)
    sizes = jnp.sum(kind[None, :] == jnp.arange(PRE + 1, dtype=jnp.int32)[:, None], axis=1)
    groups = (sizes + GROUP - 1) // GROUP
    ends = jnp.stack([groups[0], groups[0] + groups[1], groups[0] + groups[1] + groups[2]])
    begin = jnp.where(kind == 0, 0, jnp.where(kind == 1, ends[0], ends[1])) * GROUP
    index = jnp.arange(page_count, dtype=jnp.int32)
    rank = jnp.sum((kind[None, :] == kind[:, None]) & (index[None, :] < index[:, None]), axis=1)
    place = jnp.where(kind <= PRE, begin + rank, -1)
    hit = place[None, :] == jnp.arange(SLOTS, dtype=jnp.int32)[:, None]
    token = jnp.maximum(owner - PRE, 0)

    def listed(values):
        return jnp.sum(jnp.where(hit, values[None, :], 0), axis=1).astype(jnp.int32)

    last = jnp.concatenate([ends, first.astype(jnp.int32)[None]]).astype(jnp.int32)
    return jnp.stack(
        [listed(index), listed(count), listed(token), jnp.pad(last, (0, SLOTS - 4))]
    )


def join_parts(parts, heads):
    devices, tokens = parts.shape[0], parts.shape[1]
    width = heads * HD
    parts = parts.astype(jnp.float32)
    outs = parts[:, :, :width].reshape(devices, tokens, heads, HD)
    stats = parts[:, :, width : width + heads * 5].reshape(devices, tokens, heads, 5)
    maxima = stats[..., 0] + stats[..., 1] + stats[..., 2]
    share = (stats[..., 3] + stats[..., 4]) * jnp.exp((maxima - jnp.max(maxima, axis=0)) * SCALE)
    joined = jnp.sum(outs * share[..., None], axis=0) / jnp.sum(share, axis=0)[..., None]
    return joined.astype(jnp.bfloat16).reshape(tokens, width)


def shards(
    layer_input,
    norm_gain,
    qkv_weight,
    key_cache,
    value_cache,
    out_weight,
    ffn_gain,
    gate_up_weight,
    down_weight,
    span_offsets,
    decode_lengths,
    page_table,
):
    group_width = qkv_weight.shape[2]
    group_heads = group_width // HD
    n_ffn, n_grp = lax.axis_size("ffn"), lax.axis_size("grp")
    first = lax.axis_index("ffn") == 0
    page_count = key_cache.shape[0]
    plan = page_plan(
        page_table,
        span_offsets,
        decode_lengths,
        lax.axis_index("ffn") * page_count,
        page_count,
        first,
    )
    input_f32 = layer_input.astype(jnp.float32)
    scaled = (input_f32 * norm_gain[None, :]).astype(jnp.bfloat16)
    squares = jnp.sum(input_f32 * input_f32, axis=1)
    positions = token_positions(span_offsets, decode_lengths)
    partial_value = jnp.concatenate(
        [
            jnp.dot(scaled, qkv_weight[k], preferred_element_type=jnp.float32).astype(jnp.bfloat16)
            for k in range(3)
        ]
        + [jnp.broadcast_to(squares[:, None], (TOKENS, HD)).astype(jnp.bfloat16)],
        axis=1,
    )
    columns = partial_value.shape[1] // n_ffn
    own_sum = scatter_sum(
        partial_value.reshape(TOKENS, 2, n_ffn // 2, columns).transpose(1, 2, 0, 3)
    ).astype(jnp.bfloat16)
    gathered = gather_all(own_sum)
    if columns % HD == 0:
        reduced = gathered.reshape(n_ffn, TOKENS, columns)
    else:
        reduced = gathered.transpose(2, 0, 1, 3).reshape(1, TOKENS, n_ffn * columns)
    packed = attention(plan, reduced, positions, key_cache, value_cache)
    parts = lax.all_to_all(
        packed.reshape(2, n_ffn // 2, TOKENS // n_ffn, packed.shape[1])
        .swapaxes(0, 1)
        .reshape(n_ffn, TOKENS // n_ffn, packed.shape[1]),
        "ffn",
        0,
        0,
    )
    heads_out = gather_all(join_parts(parts, group_heads)).reshape(TOKENS, group_width)
    head_part = jnp.dot(heads_out, out_weight, preferred_element_type=jnp.float32)
    quarter = TOKENS // n_grp
    blocks = lax.all_to_all(
        head_part.astype(jnp.bfloat16).reshape(n_grp, quarter, head_part.shape[1]), "grp", 0, 0
    )
    own_input = lax.dynamic_slice_in_dim(layer_input, lax.axis_index("grp") * quarter, quarter, 0)
    own_block = (
        own_input.astype(jnp.float32) + jnp.sum(blocks.astype(jnp.float32), axis=0)
    ).astype(jnp.bfloat16)
    block_rows = gather_all(own_block).transpose(2, 1, 0, 3).reshape(quarter, D)
    rows_f32 = block_rows.astype(jnp.float32)
    inverse = lax.rsqrt(jnp.sum(rows_f32 * rows_f32, axis=1) / D + EPS)[:, None]
    normed = (rows_f32 * inverse * ffn_gain[None, :]).astype(jnp.bfloat16)
    gate_up = jnp.einsum("td,kdf->ktf", normed, gate_up_weight, preferred_element_type=jnp.float32)
    hidden = (jax.nn.silu(gate_up[0]) * gate_up[1]).astype(jnp.bfloat16)
    down_terms = jnp.dot(hidden, down_weight, preferred_element_type=jnp.float32)
    summed_out = scatter_sum(
        down_terms.astype(jnp.bfloat16)
        .reshape(quarter, n_ffn // 2, 2, D // n_ffn)
        .transpose(2, 1, 0, 3)
    )
    return (own_block.astype(jnp.float32) + summed_out).astype(jnp.bfloat16)


def solution(mesh):
    in_specs = (
        P(None, "ffn"),
        P("ffn"),
        P(None, "ffn", "grp"),
        P("ffn", None, "grp"),
        P("ffn", None, "grp"),
        P("grp", "ffn"),
        P(),
        P(None, None, "ffn"),
        P("ffn", None),
        P(),
        P(),
        P(),
    )
    out_specs = P("grp", "ffn")
    return jax.shard_map(shards, mesh=mesh, in_specs=in_specs, out_specs=out_specs, check_vma=False)
```
